32 devices in a mesh: section: 2 (over y), expert: 16 (over z, x, core).
Axes of the slice: x: 2, y: 2, z: 4, core: 2. Of those that a mesh axis runs over, the one named last changes fastest.
Arguments:
- inputs_fwd: bfloat16 [3840, 3584], P(('section', 'expert')), may hold values from -6 to 6
- inputs_saved: bfloat16 [3840, 3584], P(('section', 'expert')), may hold values from -6 to 6
- cotangent: bfloat16 [3840, 3584], P(('section', 'expert')), may hold values from -6 to 6
- routes_fwd: int32 [3840, 8], P(('section', 'expert')), may hold values from 0 to 255, as said below
- gates_fwd: float32 [3840, 8], P(('section', 'expert')), may hold values from 0.2 to 1
- routes_bwd: int32 [3840, 8], P(('section', 'expert')), may hold values from 0 to 255, as said below
- gates_bwd: float32 [3840, 8], P(('section', 'expert')), may hold values from 0.2 to 1
- gate_w: bfloat16 [2, 16, 448, 256], P('section', 'expert'), may hold values from -0.09375 to 0.09375
- up_w: bfloat16 [2, 16, 448, 256], P('section', 'expert'), may hold values from -0.09375 to 0.09375
- down_w: bfloat16 [2, 16, 448, 256], P('section', 'expert'), may hold values from -0.1875 to 0.1875
Outputs:
- forward_next: bfloat16 [3840, 3584], P(('section', 'expert'))
- gradient_next: bfloat16 [3840, 3584], P(('section', 'expert'))
The draws below stay inside these ranges and needn't reach their ends.
Inputs may be any that keep to these rules, and one draw needn't show every extreme that they name: `routes_fwd`: each token names 8 different experts. Among the 120 tokens of one device, each expert below 1 is named by 1 to 8 tokens; one such expert is named by exactly 8 tokens on every device. `routes_bwd`: as for routes_fwd.
All inputs are finite; a program needn't handle non-finite values.
Results may differ from the reference program's by a relative error of at most 0.0034.
Values may be sent and summed in bfloat16 or wider, within the bound.
A program may use at most 64 MiB of HBM per device.

```python
import jax
import jax.numpy as jnp
from jax import lax

D = 3584
HE = 1024
EXPERTS_ALL = 256
TOPK = 8
CAP = 8
TOK_DEV = 120
HID_DEV = 256
FLIGHT = 1
LAYERS = 1
TOKENS = 3840
N_SECTION = 2
N_EXPERT = 16


def route_table(key):
    flight = N_EXPERT // 16
    blocks = N_SECTION * N_EXPERT
    keys = jax.random.split(key, 7)
    counts = jax.random.randint(keys[0], (blocks, flight), 1, CAP + 1)
    hottest = jax.random.randint(keys[1], (), 0, flight)
    local_hot = jax.random.randint(keys[2], (blocks, 1), 0, flight)
    column = jnp.arange(flight, dtype=jnp.int32)[None, :]
    counts = jnp.where((column == hottest) | (column == local_hot), CAP, counts)
    scores = jax.random.randint(keys[3], (blocks, flight, TOK_DEV), 0, 1 << 20) * TOK_DEV + jnp.arange(TOK_DEV, dtype=jnp.int32)
    ranks = jnp.argsort(jnp.argsort(scores, axis=2), axis=2)
    member = ranks < counts[:, :, None]
    others = EXPERTS_ALL - flight
    step_most = (others - 1) // (TOPK - 1)
    start = jax.random.randint(keys[4], (blocks, TOK_DEV, 1), 0, others)
    stride = jax.random.randint(keys[5], (blocks, TOK_DEV, 1), 1, step_most + 1)
    positions = jnp.arange(TOPK, dtype=jnp.int32)
    outside = flight + (start + stride * positions) % others
    inside = jnp.transpose(member, (0, 2, 1))
    filler = jnp.zeros((blocks, TOK_DEV, TOPK - flight), dtype=bool)
    inside_full = jnp.concatenate([inside, filler], axis=2)
    named = jnp.where(inside_full, positions, outside)
    shuffle = jax.random.randint(keys[6], (blocks, TOK_DEV, TOPK), 0, 1 << 20) * TOPK + positions
    order = jnp.argsort(shuffle, axis=2)
    named = jnp.take_along_axis(named, order, axis=2)
    return named.reshape(blocks * TOK_DEV, TOPK).astype(jnp.int32)


def draw_routes_fwd(key, part):
    return route_table(jax.random.fold_in(key, 11))


def draw_routes_bwd(key, part):
    return route_table(jax.random.fold_in(key, 23))


def levels(rng, shape, shards, smallest, largest):
    level = 1.0
    for dim, parts in shards:
        heights = jax.random.uniform(jax.random.fold_in(jax.random.fold_in(rng, 6), dim), (parts,), jnp.float32, smallest / len(shards), largest / len(shards))
        level = level * jnp.repeat(jnp.exp(heights), shape[dim] // parts).reshape((-1,) + (1,) * (len(shape) - 1 - dim))
    return level


def normal_values(rng, shape, deviation, bound, cuts=(), kind=jnp.bfloat16):
    result = jax.random.normal(rng, shape, jnp.float32) * deviation
    if len(cuts) > 0:
        result = levels(rng, shape, cuts, -0.22, 0.18) * result
    return jnp.clip(result, min=-bound, max=bound).astype(kind)


def setup_inputs(seed: int = 0) -> dict:
    seeds = jax.random.split(jax.random.key(seed), 11)
    inputs_fwd = normal_values(seeds[0], (TOKENS, D), 1.0, 6.0, ((0, 32),))
    inputs_saved = normal_values(seeds[1], (TOKENS, D), 1.0, 6.0, ((0, 32),))
    cotangent = normal_values(seeds[2], (TOKENS, D), 1.0, 6.0, ((0, 32),))
    routes_fwd = draw_routes_fwd(jax.random.fold_in(seeds[10], 71), 0)
    gates_fwd = jnp.clip(0.2 + 0.8 * jax.random.uniform(seeds[4], (TOKENS, TOPK), jnp.float32) ** levels(seeds[4], (TOKENS, TOPK), ((0, 32),), -0.2, 0.2), 0.2, 1.0)
    routes_bwd = draw_routes_bwd(jax.random.fold_in(seeds[10], 71), 0)
    gates_bwd = jnp.clip(0.2 + 0.8 * jax.random.uniform(seeds[6], (TOKENS, TOPK), jnp.float32) ** levels(seeds[6], (TOKENS, TOPK), ((0, 32),), -0.2, 0.2), 0.2, 1.0)
    gate_w = normal_values(seeds[7], (N_SECTION, N_EXPERT, D // 8, HID_DEV), D ** -0.5, 0.09375, ((0, 2), (1, 16)))
    up_w = normal_values(seeds[8], (N_SECTION, N_EXPERT, D // 8, HID_DEV), D ** -0.5, 0.09375, ((0, 2), (1, 16)))
    down_w = normal_values(seeds[9], (N_SECTION, N_EXPERT, D // 8, HID_DEV), HE ** -0.5, 0.1875, ((0, 2), (1, 16)))
    return dict(inputs_fwd=inputs_fwd, inputs_saved=inputs_saved, cotangent=cotangent, routes_fwd=routes_fwd, gates_fwd=gates_fwd, routes_bwd=routes_bwd, gates_bwd=gates_bwd, gate_w=gate_w, up_w=up_w, down_w=down_w)


def tables(routes, gates):
    routes = routes.reshape(N_SECTION, N_EXPERT, TOK_DEV, TOPK)
    gates = gates.reshape(N_SECTION, N_EXPERT, TOK_DEV, TOPK)
    experts_range = jnp.arange(FLIGHT, dtype=jnp.int32)
    matches = routes[..., None] == experts_range
    member = jnp.any(matches, axis=3)
    weight_sum = jnp.sum(jnp.where(matches, gates[..., None], jnp.float32(0.0)), axis=3)
    position = jnp.cumsum(member.astype(jnp.int32), axis=2) - 1
    slots_range = jnp.arange(CAP, dtype=jnp.int32)
    chosen = member[..., None] & (position[..., None] == slots_range)
    return chosen.astype(jnp.float32), weight_sum


def select_rows(picker, values):
    blocks = values.reshape(N_SECTION, N_EXPERT, TOK_DEV, D).astype(jnp.float32)
    return jnp.einsum("pjtws,pjtd->pjwsd", picker, blocks, precision=lax.Precision.HIGHEST)


def ref_forward(rows, wg, wu, wdt):
    count = rows.shape[0]
    pre_gate = jnp.dot(rows, wg, preferred_element_type=jnp.float32)
    pre_up = jnp.dot(rows, wu, preferred_element_type=jnp.float32)
    hidden = lax.optimization_barrier((jax.nn.silu(pre_gate) * pre_up).astype(jnp.bfloat16))
    slices = jnp.einsum("nhk,dhk->nhd", hidden.reshape(count, 4, HID_DEV).astype(jnp.float32),
                        wdt.reshape(D, 4, HID_DEV).astype(jnp.float32), precision=lax.Precision.HIGHEST)
    rounded = lax.optimization_barrier(slices.astype(jnp.bfloat16))
    return jnp.sum(rounded.astype(jnp.float32), axis=1)


def ref_backward(rows, upstream, wg, wu, wdt):
    count = rows.shape[0]
    pre_gate = jnp.dot(rows, wg, preferred_element_type=jnp.float32)
    pre_up = jnp.dot(rows, wu, preferred_element_type=jnp.float32)
    sigma = jax.nn.sigmoid(pre_gate)
    activ = pre_gate * sigma
    slope = sigma * (1.0 + pre_gate * (1.0 - sigma))
    d_hidden = jnp.dot(upstream, wdt, preferred_element_type=jnp.float32)
    d_gate = lax.optimization_barrier((d_hidden * pre_up * slope).astype(jnp.bfloat16))
    d_up = lax.optimization_barrier((d_hidden * activ).astype(jnp.bfloat16))
    part = jnp.einsum("nhk,dhk->nhd", d_gate.reshape(count, 4, HID_DEV).astype(jnp.float32),
                      wg.reshape(D, 4, HID_DEV).astype(jnp.float32), precision=lax.Precision.HIGHEST)
    part = part + jnp.einsum("nhk,dhk->nhd", d_up.reshape(count, 4, HID_DEV).astype(jnp.float32),
                             wu.reshape(D, 4, HID_DEV).astype(jnp.float32), precision=lax.Precision.HIGHEST)
    rounded = lax.optimization_barrier(part.astype(jnp.bfloat16))
    return jnp.sum(rounded.astype(jnp.float32), axis=1)


def assemble_in(weight):
    shaped = weight.reshape(LAYERS, 2, FLIGHT, 4, 4, D // 8, HID_DEV)
    return shaped.transpose(0, 2, 1, 4, 5, 3, 6).reshape(LAYERS, FLIGHT, D, HE)


def reference(inputs_fwd, inputs_saved, cotangent, routes_fwd, gates_fwd, routes_bwd, gates_bwd, gate_w, up_w, down_w):
    wg_all = assemble_in(gate_w)
    wu_all = assemble_in(up_w)
    wdt_all = assemble_in(down_w)
    pick_fwd, weight_fwd = tables(routes_fwd, gates_fwd)
    pick_bwd, weight_bwd = tables(routes_bwd, gates_bwd)
    rows_fwd = select_rows(pick_fwd, inputs_fwd).astype(jnp.bfloat16)
    rows_bwd = select_rows(pick_bwd, inputs_saved).astype(jnp.bfloat16)
    upstream = select_rows(pick_bwd * weight_bwd[..., None], cotangent).astype(jnp.bfloat16)
    layer_fwd = []
    layer_bwd = []
    for layer in range(LAYERS):
        outs_fwd = []
        outs_bwd = []
        for expert in range(FLIGHT):
            block_fwd = rows_fwd[2 * layer:2 * layer + 2, :, expert].reshape(-1, D)
            block_bwd = rows_bwd[2 * layer:2 * layer + 2, :, expert].reshape(-1, D)
            block_up = upstream[2 * layer:2 * layer + 2, :, expert].reshape(-1, D)
            wg = wg_all[layer, expert]
            wu = wu_all[layer, expert]
            wdt = wdt_all[layer, expert]
            outs_fwd.append(ref_forward(block_fwd, wg, wu, wdt).reshape(2, N_EXPERT, CAP, D))
            outs_bwd.append(ref_backward(block_bwd, block_up, wg, wu, wdt).reshape(2, N_EXPERT, CAP, D))
        layer_fwd.append(jnp.stack(outs_fwd, axis=2))
        layer_bwd.append(jnp.stack(outs_bwd, axis=2))
    expert_out = jnp.concatenate(layer_fwd, axis=0)
    expert_back = jnp.concatenate(layer_bwd, axis=0)
    branch = jnp.einsum("pjtws,pjwsd->pjtd", pick_fwd * weight_fwd[..., None], expert_out,
                        precision=lax.Precision.HIGHEST)
    layer_out = (inputs_fwd.reshape(N_SECTION, N_EXPERT, TOK_DEV, D).astype(jnp.float32) + branch).astype(jnp.bfloat16)
    carried = jnp.einsum("pjtws,pjwsd->pjtd", pick_bwd, expert_back, precision=lax.Precision.HIGHEST)
    input_grad = (cotangent.reshape(N_SECTION, N_EXPERT, TOK_DEV, D).astype(jnp.float32) + carried).astype(jnp.bfloat16)
    forward_next = jnp.roll(layer_out, 2, axis=0).reshape(TOKENS, D)
    gradient_next = jnp.roll(input_grad, -2, axis=0).reshape(TOKENS, D)
    return forward_next, gradient_next
```

```python
import functools

import jax
import jax.numpy as jnp
from jax import lax
from jax.experimental import pallas as pl
from jax.experimental.pallas import tpu as pltpu
from jax.sharding import PartitionSpec as P

CAP = 8
SLICES = 4
HID = 256
MESH = pl.DeviceIdType.MESH
F32 = jnp.float32
BF16 = jnp.bfloat16
NT = (((1,), (1,)), ((), ()))


def member_of(routes, gates, e, width):
    tokens = routes.shape[0]
    match = routes == e
    member = jnp.max(match.astype(F32), axis=1, keepdims=True)
    masked = jnp.where(match, gates, 0.0)
    tri = (
        lax.broadcasted_iota(jnp.int32, (tokens, tokens), 0)
        >= lax.broadcasted_iota(jnp.int32, (tokens, tokens), 1)
    ).astype(F32).astype(BF16)
    wide = jnp.broadcast_to(member, (tokens, width)).astype(BF16)
    position = jnp.dot(tri, wide, preferred_element_type=F32) - 1.0
    slot = (lax.broadcasted_iota(jnp.int32, (tokens, width), 1) % CAP).astype(F32)
    chosen = jnp.where((position == slot) & (wide > 0), 1.0, 0.0)
    return chosen, masked


def transposed(chosen):
    eye = (
        lax.broadcasted_iota(jnp.int32, (CAP, CAP), 0)
        == lax.broadcasted_iota(jnp.int32, (CAP, CAP), 1)
    ).astype(F32).astype(BF16)
    return lax.dot_general(eye, chosen.astype(BF16), NT, preferred_element_type=F32)


def kernel(
    n_expert, chunk,
    x_ref, s_ref, g_ref, rf_ref, gf_ref, rb_ref, gb_ref, gw_ref, uw_ref, dw_ref,
    of_ref, ob_ref,
    send_f, send_b, in_f, in_b, w, p32_f, p32_b, ps_f, ps_b, pr_f, pr_b, h_f, h_b,
    o_f, o_b, r_f, r_b,
    w_s, w_r, inf_s, inf_r, inb_s, inb_r, pf_s, pf_r, pb_s, pb_r, hf_s, hf_r, hb_s, hb_r,
    of_s, of_r, ob_s, ob_r,
):
    flight = n_expert // 16
    group = n_expert
    half = group // 2
    rows = group // 4 * CAP
    section, expert = lax.axis_index("section"), lax.axis_index("expert")
    layer, c, k = section // 2, section % 2, expert % 2
    place = expert // 2
    me = c * half + place
    x = place % 2
    h = place // 2 % 4
    e_here = place // 8
    q = 2 * c + x

    def device(n):
        return (layer * 2 + n // half, (n % half) * 2 + k)

    def quad_device(other):
        return (layer * 2 + other // 2, e_here * 16 + h * 4 + (other % 2) * 2 + k)

    partner = (section, expert + 1 - 2 * k)

    barrier = pltpu.get_barrier_semaphore()
    pl.semaphore_signal(barrier, inc=1, device_id=partner, device_id_type=MESH)

    def greet(d, carry):
        pl.semaphore_signal(
            barrier, inc=1, device_id=device((me + d) % group), device_id_type=MESH
        )
        return carry

    lax.fori_loop(1, group, greet, 0)

    def scatter(src, dst, ssem, rsem):
        def body(d, carry):
            n = (me + d) % group
            spot = n % half
            pltpu.make_async_remote_copy(
                src_ref=src(n, spot // 8, 2 * (n // half) + spot % 2),
                dst_ref=dst, send_sem=ssem.at[n], recv_sem=rsem.at[me],
                device_id=device(n), device_id_type=MESH,
            ).start()
            return carry

        lax.fori_loop(1, group, body, 0)

    def gathered(src, dst, ssem, rsem):
        def body(d, carry):
            n = (me + d) % group
            pltpu.make_async_remote_copy(
                src_ref=src, dst_ref=dst(n), send_sem=ssem.at[n], recv_sem=rsem.at[n],
                device_id=device(n), device_id_type=MESH,
            ).wait_recv()
            return carry

        lax.fori_loop(1, group, body, 0)

    def drained(src, dst, ssem, rsem):
        def body(d, carry):
            n = (me + d) % group
            pltpu.make_async_remote_copy(
                src_ref=src, dst_ref=dst, send_sem=ssem.at[n], recv_sem=rsem.at[n],
                device_id=device(n), device_id_type=MESH,
            ).wait_send()
            return carry

        lax.fori_loop(1, group, body, 0)

    def quad_copy(src, dst, ssem, rsem, d):
        return pltpu.make_async_remote_copy(
            src_ref=src, dst_ref=dst, send_sem=ssem.at[d], recv_sem=rsem.at[d],
            device_id=quad_device((q + d) % 4), device_id_type=MESH,
        )

    for e in range(flight):
        chosen, _ = member_of(rf_ref[...], gf_ref[...], e, CAP)
        pick = transposed(chosen).astype(BF16)
        for part in range(4):
            cols = slice(part * chunk, (part + 1) * chunk)
            send_f[e, part] = jnp.dot(pick, x_ref[:, cols], preferred_element_type=F32).astype(BF16)

    pl.semaphore_wait(barrier, group)
    scatter(lambda n, e, part: send_f.at[e, part], in_f.at[me], inf_s, inf_r)
    weight_copies = []
    for i, ref in enumerate((gw_ref, uw_ref, dw_ref)):
        copy = pltpu.make_async_remote_copy(
            src_ref=ref.at[0, 0], dst_ref=w.at[i, k], send_sem=w_s.at[i], recv_sem=w_r.at[i],
            device_id=partner, device_id_type=MESH,
        )
        copy.start()
        weight_copies.append(copy)

    for e in range(flight):
        chosen, masked = member_of(rb_ref[...], gb_ref[...], e, CAP)
        pick_f32 = transposed(chosen)
        pick = pick_f32.astype(BF16)
        weight = lax.dot_general(
            jnp.ones((CAP, masked.shape[1]), F32), masked, NT,
            precision=lax.Precision.HIGHEST, preferred_element_type=F32,
        )
        gate = jnp.sum(pick_f32 * weight, axis=1, keepdims=True)
        for part in range(4):
            cols = slice(part * chunk, (part + 1) * chunk)
            send_b[e, part, 0] = jnp.dot(pick, s_ref[:, cols], preferred_element_type=F32).astype(BF16)
            picked = jnp.dot(pick, g_ref[:, cols], preferred_element_type=F32)
            send_b[e, part, 1] = (picked * gate).astype(BF16)
    scatter(lambda n, e, part: send_b.at[e, part], in_b.at[me], inb_s, inb_r)

    in_f[me] = send_f[e_here, q]
    in_b[me] = send_b[e_here, q]
    for i, ref in enumerate((gw_ref, uw_ref, dw_ref)):
        w[i, k] = ref[0, 0]
    for copy in weight_copies:
        copy.wait_recv()

    def matrix(i):
        return w[i].reshape(chunk, HID)

    def flat(block):
        return block.astype(F32).reshape(group * CAP, chunk).astype(BF16)

    def reduce_part(p32, ps, pr, ssem, rsem):
        copies = [quad_copy(ps.at[(q + d) % 4], pr.at[d], ssem, rsem, d) for d in range(1, 4)]
        for copy in copies:
            copy.start()
        total = p32[q]
        for d in range(1, 4):
            copies[d - 1].wait_recv()
            total = total + pr[d].astype(F32)
        return total, copies

    def share(h_ref, value, ssem, rsem):
        h_ref[q] = value
        copies = [quad_copy(h_ref.at[q], h_ref.at[q], ssem, rsem, d) for d in range(1, 4)]
        for copy in copies:
            copy.start()
        for d in range(1, 4):
            quad_copy(h_ref.at[q], h_ref.at[(q - d + 4) % 4], ssem, rsem, d).wait_recv()
        return copies

    gathered(send_f.at[0, 0], lambda n: in_f.at[n], inf_s, inf_r)
    block = flat(in_f[...])
    for i in range(2):
        part = jnp.dot(block, matrix(i), preferred_element_type=F32).reshape(4, rows, HID)
        p32_f[:, :, i * HID:(i + 1) * HID] = part
        ps_f[:, :, i * HID:(i + 1) * HID] = part.astype(BF16)
    total, sent_pf = reduce_part(p32_f, ps_f, pr_f, pf_s, pf_r)
    a, b = total[:, :HID], total[:, HID:]
    sent_hf = share(h_f, (a * jax.nn.sigmoid(a) * b).astype(BF16), hf_s, hf_r)
    hidden = h_f[...].reshape(group * CAP, HID)
    o_f[...] = (
        lax.dot_general(hidden, matrix(2), NT, preferred_element_type=F32)
        .reshape(group, CAP, chunk).astype(BF16)
    )
    scatter(lambda n, e, part: o_f.at[n], r_f.at[c, e_here, h, x], of_s, of_r)
    r_f[c, e_here, h, x] = o_f[me]

    gathered(send_b.at[0, 0], lambda n: in_b.at[n], inb_s, inb_r)
    block = flat(in_b[:, 0])
    for i in range(3):
        if i == 2:
            block = flat(in_b[:, 1])
        part = jnp.dot(block, matrix(i), preferred_element_type=F32).reshape(4, rows, HID)
        p32_b[:, :, i * HID:(i + 1) * HID] = part
        ps_b[:, :, i * HID:(i + 1) * HID] = part.astype(BF16)
    total, sent_pb = reduce_part(p32_b, ps_b, pr_b, pb_s, pb_r)
    a, b, d_hidden = total[:, :HID], total[:, HID:2 * HID], total[:, 2 * HID:]
    sigma = jax.nn.sigmoid(a)
    d_gate = (d_hidden * b * (sigma * (1.0 + a * (1.0 - sigma)))).astype(BF16)
    d_up = (d_hidden * (a * sigma)).astype(BF16)
    sent_hb = share(h_b, jnp.concatenate([d_gate, d_up], axis=1), hb_s, hb_r)
    both = h_b[...].reshape(group * CAP, 2 * HID)
    back = lax.dot_general(both[:, :HID], matrix(0), NT, preferred_element_type=F32)
    back = back + lax.dot_general(both[:, HID:], matrix(1), NT, preferred_element_type=F32)
    o_b[...] = back.reshape(group, CAP, chunk).astype(BF16)
    scatter(lambda n, e, part: o_b.at[n], r_b.at[c, e_here, h, x], ob_s, ob_r)
    r_b[c, e_here, h, x] = o_b[me]

    def combine(routes, gates, base, returned, out, weighted):
        picks = []
        for e in range(flight):
            chosen, masked = member_of(routes[...], gates[...], e, SLICES * CAP)
            picks.append((chosen.astype(BF16), jnp.sum(masked, axis=1, keepdims=True)))
        for part in range(4):
            cols = slice(part * chunk, (part + 1) * chunk)
            total = base[:, cols].astype(F32)
            for e in range(flight):
                chosen, weight = picks[e]
                piece = returned[part // 2, e, :, part % 2].astype(F32)
                piece = piece.reshape(SLICES * CAP, chunk).astype(BF16)
                term = jnp.dot(chosen, piece, preferred_element_type=F32)
                total = total + (term * weight if weighted else term)
            out[:, cols] = total.astype(BF16)

    def slot_of(buffer):
        return lambda n: buffer.at[n // half, n % half // 8, n % half // 2 % 4, n % 2]

    gathered(o_f.at[0], slot_of(r_f), of_s, of_r)
    combine(rf_ref, gf_ref, x_ref, r_f, of_ref, True)
    gathered(o_b.at[0], slot_of(r_b), ob_s, ob_r)
    combine(rb_ref, gb_ref, g_ref, r_b, ob_ref, False)

    drained(send_f.at[0, 0], in_f.at[0], inf_s, inf_r)
    drained(send_b.at[0, 0], in_b.at[0], inb_s, inb_r)
    drained(o_f.at[0], r_f.at[0, 0, 0, 0], of_s, of_r)
    drained(o_b.at[0], r_b.at[0, 0, 0, 0], ob_s, ob_r)
    for copy in weight_copies + sent_pf + sent_hf + sent_pb + sent_hb:
        copy.wait_send()


def solution(mesh):
    n_expert, n_section = mesh.shape["expert"], mesh.shape["section"]
    flight, group = n_expert // 16, n_expert
    tokens_spec = P(("section", "expert"), None)
    weight_spec = P("section", "expert", None, None)

    def per_device(*args):
        x = args[0]
        chunk = x.shape[1] // 4
        rows = group // 4 * CAP
        vmem = pl.BlockSpec(memory_space=pltpu.VMEM)
        dma = pltpu.SemaphoreType.DMA
        scratch = [
            pltpu.VMEM((flight, 4, CAP, chunk), BF16),
            pltpu.VMEM((flight, 4, 2, CAP, chunk), BF16),
            pltpu.VMEM((group, CAP, chunk), BF16),
            pltpu.VMEM((group, 2, CAP, chunk), BF16),
            pltpu.VMEM((3, 2, chunk // 2, HID), BF16),
            pltpu.VMEM((4, rows, 2 * HID), F32),
            pltpu.VMEM((4, rows, 3 * HID), F32),
            pltpu.VMEM((4, rows, 2 * HID), BF16),
            pltpu.VMEM((4, rows, 3 * HID), BF16),
            pltpu.VMEM((4, rows, 2 * HID), BF16),
            pltpu.VMEM((4, rows, 3 * HID), BF16),
            pltpu.VMEM((4, rows, HID), BF16),
            pltpu.VMEM((4, rows, 2 * HID), BF16),
            pltpu.VMEM((group, CAP, chunk), BF16),
            pltpu.VMEM((group, CAP, chunk), BF16),
            pltpu.VMEM((2, flight, SLICES, 2, CAP, chunk), BF16),
            pltpu.VMEM((2, flight, SLICES, 2, CAP, chunk), BF16),
            dma((3,)), dma((3,)),
            dma((group,)), dma((group,)), dma((group,)), dma((group,)),
            dma((4,)), dma((4,)), dma((4,)), dma((4,)),
            dma((4,)), dma((4,)), dma((4,)), dma((4,)),
            dma((group,)), dma((group,)), dma((group,)), dma((group,)),
        ]
        out = jax.ShapeDtypeStruct(x.shape, BF16)
        forward, gradient = pl.pallas_call(
            functools.partial(kernel, n_expert, chunk),
            out_shape=(out, out),
            in_specs=[vmem] * 10,
            out_specs=(vmem, vmem),
            scratch_shapes=scratch,
            compiler_params=pltpu.CompilerParams(
                collective_id=0, has_side_effects=True, vmem_limit_bytes=48 * 1024 * 1024
            ),
        )(*args)
        if n_section > 2:
            onward = [(i, (i + 2) % n_section) for i in range(n_section)]
            back = [(i, (i - 2) % n_section) for i in range(n_section)]
            forward = lax.ppermute(forward, "section", onward)
            gradient = lax.ppermute(gradient, "section", back)
        return forward, gradient

    return jax.shard_map(
        per_device,
        mesh=mesh,
        in_specs=(tokens_spec,) * 7 + (weight_spec,) * 3,
        out_specs=(tokens_spec, tokens_spec),
        check_vma=False,
    )
```

```python
import functools

import jax
import jax.numpy as jnp
from jax import lax
from jax.experimental import pallas as pl
from jax.experimental.pallas import tpu as pltpu
from jax.sharding import PartitionSpec as P

CAP = 8
SLICES = 4
HID = 256
MESH = pl.DeviceIdType.MESH
F32 = jnp.float32
BF16 = jnp.bfloat16
NT = (((1,), (1,)), ((), ()))


def eye(size, dtype):
    rows = lax.broadcasted_iota(jnp.int32, (size, size), 0)
    cols = lax.broadcasted_iota(jnp.int32, (size, size), 1)
    return (rows == cols).astype(F32).astype(dtype)


def chosen_of(routes, e, height):
    tokens = routes.shape[1]
    member = jnp.max((routes == e).astype(F32), axis=0, keepdims=True)
    tri = (
        lax.broadcasted_iota(jnp.int32, (tokens, tokens), 0)
        >= lax.broadcasted_iota(jnp.int32, (tokens, tokens), 1)
    ).astype(F32).astype(BF16)
    wide = jnp.broadcast_to(member, (height, tokens))
    position = lax.dot_general(wide.astype(BF16), tri, NT, preferred_element_type=F32) - 1.0
    slot = (lax.broadcasted_iota(jnp.int32, (height, tokens), 0) % CAP).astype(F32)
    return jnp.where((position == slot) & (wide > 0), 1.0, 0.0)


def gate_of(routes, gates, e):
    return jnp.sum(jnp.where(routes == e, gates, 0.0), axis=0, keepdims=True)


def kernel(
    n_expert, chunk,
    x_hbm, s_hbm, g_hbm, rf_hbm, gf_hbm, rb_hbm, gb_hbm, gw_ref, uw_ref, dw_ref,
    of_hbm, ob_hbm,
    x_ref, s_ref, g_ref, rf_ref, gf_ref, rb_ref, gb_ref, load, of_ref, ob_ref, store,
    send_f, send_b, in_f, in_b, w, p32_f, p32_b, ps_f, ps_b, pr_f, pr_b, h_f, h_b,
    o_f, o_b, r_f, r_b,
    w_s, w_r, inf_s, inf_r, inb_s, inb_r, pf_s, pf_r, pb_s, pb_r, hf_s, hf_r, hb_s, hb_r,
    of_s, of_r, ob_s, ob_r,
):
    flight = n_expert // 16
    group = n_expert
    half = group // 2
    rows = group // 4 * CAP
    section, expert = lax.axis_index("section"), lax.axis_index("expert")
    layer, c, k = section // 2, section % 2, expert % 2
    place = expert // 2
    me = c * half + place
    x = place % 2
    h = place // 2 % 4
    e_here = place // 8
    q = 2 * c + x

    def device(n):
        return (layer * 2 + n // half, (n % half) * 2 + k)

    def quad_device(other):
        return (layer * 2 + other // 2, e_here * 16 + h * 4 + (other % 2) * 2 + k)

    loads = [
        pltpu.make_async_copy(src, dst, load.at[i])
        for i, (src, dst) in enumerate((
            (rf_hbm, rf_ref), (x_hbm, x_ref), (rb_hbm, rb_ref), (gb_hbm, gb_ref),
            (s_hbm, s_ref), (g_hbm, g_ref), (gf_hbm, gf_ref),
            (gw_ref.at[0, 0], w.at[0, k]), (uw_ref.at[0, 0], w.at[1, k]),
            (dw_ref.at[0, 0], w.at[2, k]),
        ))
    ]
    for copy in loads:
        copy.start()

    partner = (section, expert + 1 - 2 * k)

    barrier = pltpu.get_barrier_semaphore()
    pl.semaphore_signal(barrier, inc=1, device_id=partner, device_id_type=MESH)

    def greet(d, carry):
        pl.semaphore_signal(
            barrier, inc=1, device_id=device((me + d) % group), device_id_type=MESH
        )
        return carry

    lax.fori_loop(1, group, greet, 0)

    def scatter(src, dst, ssem, rsem):
        def body(d, carry):
            n = (me + d) % group
            spot = n % half
            pltpu.make_async_remote_copy(
                src_ref=src(n, spot // 8, 2 * (n // half) + spot % 2),
                dst_ref=dst, send_sem=ssem.at[n], recv_sem=rsem.at[me],
                device_id=device(n), device_id_type=MESH,
            ).start()
            return carry

        lax.fori_loop(1, group, body, 0)

    def gathered(src, dst, ssem, rsem):
        def body(d, carry):
            n = (me + d) % group
            pltpu.make_async_remote_copy(
                src_ref=src, dst_ref=dst(n), send_sem=ssem.at[n], recv_sem=rsem.at[n],
                device_id=device(n), device_id_type=MESH,
            ).wait_recv()
            return carry

        lax.fori_loop(1, group, body, 0)

    def drained(src, dst, ssem, rsem):
        def body(d, carry):
            n = (me + d) % group
            pltpu.make_async_remote_copy(
                src_ref=src, dst_ref=dst, send_sem=ssem.at[n], recv_sem=rsem.at[n],
                device_id=device(n), device_id_type=MESH,
            ).wait_send()
            return carry

        lax.fori_loop(1, group, body, 0)

    def quad_copy(src, dst, ssem, rsem, d):
        return pltpu.make_async_remote_copy(
            src_ref=src, dst_ref=dst, send_sem=ssem.at[d], recv_sem=rsem.at[d],
            device_id=quad_device((q + d) % 4), device_id_type=MESH,
        )

    loads[0].wait()
    picks_f = [chosen_of(rf_ref[...], e, CAP).astype(BF16) for e in range(flight)]
    loads[1].wait()
    for e in range(flight):
        pick = picks_f[e]
        for part in range(4):
            cols = slice(part * chunk, (part + 1) * chunk)
            send_f[e, part] = jnp.dot(pick, x_ref[:, cols], preferred_element_type=F32).astype(BF16)

    pl.semaphore_wait(barrier, group)
    scatter(lambda n, e, part: send_f.at[e, part], in_f.at[me], inf_s, inf_r)
    weight_copies = []
    for i, ref in enumerate((gw_ref, uw_ref, dw_ref)):
        copy = pltpu.make_async_remote_copy(
            src_ref=ref.at[0, 0], dst_ref=w.at[i, k], send_sem=w_s.at[i], recv_sem=w_r.at[i],
            device_id=partner, device_id_type=MESH,
        )
        copy.start()
        weight_copies.append(copy)

    for copy in loads[2:6]:
        copy.wait()
    for e in range(flight):
        pick_f32 = chosen_of(rb_ref[...], e, CAP)
        pick = pick_f32.astype(BF16)
        weight = gate_of(rb_ref[...], gb_ref[...], e)
        gate = jnp.sum(pick_f32 * weight, axis=1, keepdims=True)
        for part in range(4):
            cols = slice(part * chunk, (part + 1) * chunk)
            send_b[e, part, 0] = jnp.dot(pick, s_ref[:, cols], preferred_element_type=F32).astype(BF16)
            picked = jnp.dot(pick, g_ref[:, cols], preferred_element_type=F32)
            send_b[e, part, 1] = (picked * gate).astype(BF16)
    scatter(lambda n, e, part: send_b.at[e, part], in_b.at[me], inb_s, inb_r)

    in_f[me] = send_f[e_here, q]
    in_b[me] = send_b[e_here, q]
    for copy in loads[6:]:
        copy.wait()
    for copy in weight_copies:
        copy.wait_recv()

    def matrix(i):
        return w[i].reshape(chunk, HID)

    def flat(block):
        return block.astype(F32).reshape(group * CAP, chunk).astype(BF16)

    def reduce_part(p32, ps, pr, ssem, rsem):
        copies = [quad_copy(ps.at[(q + d) % 4], pr.at[d], ssem, rsem, d) for d in range(1, 4)]
        for copy in copies:
            copy.start()
        total = p32[q]
        for d in range(1, 4):
            copies[d - 1].wait_recv()
            total = total + pr[d].astype(F32)
        return total, copies

    def share(h_ref, value, ssem, rsem):
        h_ref[q] = value
        copies = [quad_copy(h_ref.at[q], h_ref.at[q], ssem, rsem, d) for d in range(1, 4)]
        for copy in copies:
            copy.start()
        for d in range(1, 4):
            quad_copy(h_ref.at[q], h_ref.at[(q - d + 4) % 4], ssem, rsem, d).wait_recv()
        return copies

    gathered(send_f.at[0, 0], lambda n: in_f.at[n], inf_s, inf_r)
    block = flat(in_f[...])
    for i in range(2):
        part = jnp.dot(block, matrix(i), preferred_element_type=F32).reshape(4, rows, HID)
        p32_f[:, :, i * HID:(i + 1) * HID] = part
        ps_f[:, :, i * HID:(i + 1) * HID] = part.astype(BF16)
    total, sent_pf = reduce_part(p32_f, ps_f, pr_f, pf_s, pf_r)
    a, b = total[:, :HID], total[:, HID:]
    sent_hf = share(h_f, (a * jax.nn.sigmoid(a) * b).astype(BF16), hf_s, hf_r)
    hidden = h_f[...].reshape(group * CAP, HID)
    o_f[...] = (
        lax.dot_general(hidden, matrix(2), NT, preferred_element_type=F32)
        .reshape(group, CAP, chunk).astype(BF16)
    )
    scatter(lambda n, e, part: o_f.at[n], r_f.at[c, e_here, h, x], of_s, of_r)
    r_f[c, e_here, h, x] = o_f[me]

    gathered(send_b.at[0, 0], lambda n: in_b.at[n], inb_s, inb_r)
    block = flat(in_b[:, 0])
    for i in range(3):
        if i == 2:
            block = flat(in_b[:, 1])
        part = jnp.dot(block, matrix(i), preferred_element_type=F32).reshape(4, rows, HID)
        p32_b[:, :, i * HID:(i + 1) * HID] = part
        ps_b[:, :, i * HID:(i + 1) * HID] = part.astype(BF16)
    total, sent_pb = reduce_part(p32_b, ps_b, pr_b, pb_s, pb_r)
    a, b, d_hidden = total[:, :HID], total[:, HID:2 * HID], total[:, 2 * HID:]
    sigma = jax.nn.sigmoid(a)
    d_gate = (d_hidden * b * (sigma * (1.0 + a * (1.0 - sigma)))).astype(BF16)
    d_up = (d_hidden * (a * sigma)).astype(BF16)
    sent_hb = share(h_b, jnp.concatenate([d_gate, d_up], axis=1), hb_s, hb_r)
    both = h_b[...].reshape(group * CAP, 2 * HID)
    back = lax.dot_general(both[:, :HID], matrix(0), NT, preferred_element_type=F32)
    back = back + lax.dot_general(both[:, HID:], matrix(1), NT, preferred_element_type=F32)
    o_b[...] = back.reshape(group, CAP, chunk).astype(BF16)
    scatter(lambda n, e, part: o_b.at[n], r_b.at[c, e_here, h, x], ob_s, ob_r)
    r_b[c, e_here, h, x] = o_b[me]

    def combine(routes, gates, base, returned, out, out_hbm, weighted):
        picks = []
        stores = []
        for e in range(flight):
            tokens = routes.shape[1]
            chosen = chosen_of(routes[...], e, SLICES * CAP).astype(BF16)
            chosen = lax.dot_general(eye(tokens, BF16), chosen, NT, preferred_element_type=F32)
            gate = None
            if weighted:
                gate = lax.dot_general(
                    eye(tokens, F32), jnp.broadcast_to(gate_of(routes[...], gates[...], e), (CAP, tokens)),
                    NT, precision=lax.Precision.HIGHEST, preferred_element_type=F32,
                )[:, :1]
            picks.append((chosen.astype(BF16), gate))
        for part in range(4):
            cols = slice(part * chunk, (part + 1) * chunk)
            total = base[:, cols].astype(F32)
            for e in range(flight):
                chosen, weight = picks[e]
                piece = returned[part // 2, e, :, part % 2].astype(F32)
                piece = piece.reshape(SLICES * CAP, chunk).astype(BF16)
                term = jnp.dot(chosen, piece, preferred_element_type=F32)
                total = total + (term * weight if weighted else term)
            out[:, cols] = total.astype(BF16)
            stores.append(pltpu.make_async_copy(
                out.at[:, cols], out_hbm.at[:, cols], store.at[0 if weighted else 1, part]
            ))
            stores[-1].start()
        return stores

    def slot_of(buffer):
        return lambda n: buffer.at[n // half, n % half // 8, n % half // 2 % 4, n % 2]

    gathered(o_f.at[0], slot_of(r_f), of_s, of_r)
    stores = combine(rf_ref, gf_ref, x_ref, r_f, of_ref, of_hbm, True)
    gathered(o_b.at[0], slot_of(r_b), ob_s, ob_r)
    stores += combine(rb_ref, gb_ref, g_ref, r_b, ob_ref, ob_hbm, False)

    drained(send_f.at[0, 0], in_f.at[0], inf_s, inf_r)
    drained(send_b.at[0, 0], in_b.at[0], inb_s, inb_r)
    drained(o_f.at[0], r_f.at[0, 0, 0, 0], of_s, of_r)
    drained(o_b.at[0], r_b.at[0, 0, 0, 0], ob_s, ob_r)
    for copy in weight_copies + sent_pf + sent_hf + sent_pb + sent_hb:
        copy.wait_send()
    for copy in stores:
        copy.wait()


def solution(mesh):
    n_expert, n_section = mesh.shape["expert"], mesh.shape["section"]
    flight, group = n_expert // 16, n_expert
    tokens_spec = P(("section", "expert"), None)
    weight_spec = P("section", "expert", None, None)

    def per_device(*args):
        x = args[0]
        args = args[:3] + tuple(a.T for a in args[3:7]) + args[7:]
        chunk = x.shape[1] // 4
        rows = group // 4 * CAP
        hbm = pl.BlockSpec(memory_space=pltpu.HBM)
        dma = pltpu.SemaphoreType.DMA
        scratch = [
            pltpu.VMEM(x.shape, BF16), pltpu.VMEM(x.shape, BF16), pltpu.VMEM(x.shape, BF16),
            *[pltpu.VMEM(a.shape, a.dtype) for a in args[3:7]],
            dma((10,)),
            pltpu.VMEM(x.shape, BF16), pltpu.VMEM(x.shape, BF16), dma((2, 4)),
            pltpu.VMEM((flight, 4, CAP, chunk), BF16),
            pltpu.VMEM((flight, 4, 2, CAP, chunk), BF16),
            pltpu.VMEM((group, CAP, chunk), BF16),
            pltpu.VMEM((group, 2, CAP, chunk), BF16),
            pltpu.VMEM((3, 2, chunk // 2, HID), BF16),
            pltpu.VMEM((4, rows, 2 * HID), F32),
            pltpu.VMEM((4, rows, 3 * HID), F32),
            pltpu.VMEM((4, rows, 2 * HID), BF16),
            pltpu.VMEM((4, rows, 3 * HID), BF16),
            pltpu.VMEM((4, rows, 2 * HID), BF16),
            pltpu.VMEM((4, rows, 3 * HID), BF16),
            pltpu.VMEM((4, rows, HID), BF16),
            pltpu.VMEM((4, rows, 2 * HID), BF16),
            pltpu.VMEM((group, CAP, chunk), BF16),
            pltpu.VMEM((group, CAP, chunk), BF16),
            pltpu.VMEM((2, flight, SLICES, 2, CAP, chunk), BF16),
            pltpu.VMEM((2, flight, SLICES, 2, CAP, chunk), BF16),
            dma((3,)), dma((3,)),
            dma((group,)), dma((group,)), dma((group,)), dma((group,)),
            dma((4,)), dma((4,)), dma((4,)), dma((4,)),
            dma((4,)), dma((4,)), dma((4,)), dma((4,)),
            dma((group,)), dma((group,)), dma((group,)), dma((group,)),
        ]
        out = jax.ShapeDtypeStruct(x.shape, BF16)
        forward, gradient = pl.pallas_call(
            functools.partial(kernel, n_expert, chunk),
            out_shape=(out, out),
            in_specs=[hbm] * 10,
            out_specs=(hbm, hbm),
            scratch_shapes=scratch,
            compiler_params=pltpu.CompilerParams(
                collective_id=0, has_side_effects=True, vmem_limit_bytes=58 * 1024 * 1024
            ),
        )(*args)
        if n_section > 2:
            onward = [(i, (i + 2) % n_section) for i in range(n_section)]
            back = [(i, (i - 2) % n_section) for i in range(n_section)]
            forward = lax.ppermute(forward, "section", onward)
            gradient = lax.ppermute(gradient, "section", back)
        return forward, gradient

    return jax.shard_map(
        per_device,
        mesh=mesh,
        in_specs=(tokens_spec,) * 7 + (weight_spec,) * 3,
        out_specs=(tokens_spec, tokens_spec),
        check_vma=False,
    )
```

```python
import functools

import jax
import jax.numpy as jnp
from jax import lax
from jax.experimental import pallas as pl
from jax.experimental.pallas import tpu as pltpu
from jax.sharding import PartitionSpec as P

CAP = 8
SLICES = 4
HID = 256
MESH = pl.DeviceIdType.MESH
F32 = jnp.float32
BF16 = jnp.bfloat16
NT = (((1,), (1,)), ((), ()))


def eye(size, dtype):
    rows = lax.broadcasted_iota(jnp.int32, (size, size), 0)
    cols = lax.broadcasted_iota(jnp.int32, (size, size), 1)
    return (rows == cols).astype(F32).astype(dtype)


def chosen_of(routes, e, height):
    tokens = routes.shape[1]
    member = jnp.max((routes == e).astype(F32), axis=0, keepdims=True)
    tri = (
        lax.broadcasted_iota(jnp.int32, (tokens, tokens), 0)
        >= lax.broadcasted_iota(jnp.int32, (tokens, tokens), 1)
    ).astype(F32).astype(BF16)
    wide = jnp.broadcast_to(member, (height, tokens))
    position = lax.dot_general(wide.astype(BF16), tri, NT, preferred_element_type=F32) - 1.0
    slot = (lax.broadcasted_iota(jnp.int32, (height, tokens), 0) % CAP).astype(F32)
    return jnp.where((position == slot) & (wide > 0), 1.0, 0.0)


def gate_of(routes, gates, e):
    return jnp.sum(jnp.where(routes == e, gates, 0.0), axis=0, keepdims=True)


def kernel(
    n_expert, chunk,
    x_hbm, s_hbm, g_hbm, rf_hbm, gf_hbm, rb_hbm, gb_hbm, gw_ref, uw_ref, dw_ref,
    of_hbm, ob_hbm,
    x_ref, s_ref, g_ref, rf_ref, gf_ref, rb_ref, gb_ref, load, of_ref, ob_ref, store,
    send_f, send_b, in_f, in_b, w, p32_f, p32_b, ps_f, ps_b, pr_f, pr_b, h_f, h_b,
    o_f, o_b, r_f, r_b,
    w_s, w_r, inf_s, inf_r, inb_s, inb_r, pf_s, pf_r, pb_s, pb_r, hf_s, hf_r, hb_s, hb_r,
    of_s, of_r, ob_s, ob_r,
):
    flight = n_expert // 16
    group = n_expert
    half = group // 2
    rows = group // 4 * CAP
    section, expert = lax.axis_index("section"), lax.axis_index("expert")
    layer, c, k = section // 2, section % 2, expert % 2
    place = expert // 2
    me = c * half + place
    x = place % 2
    h = place // 2 % 4
    e_here = place // 8
    q = 2 * c + x

    def device(n):
        return (layer * 2 + n // half, (n % half) * 2 + k)

    def quad_device(other):
        return (layer * 2 + other // 2, e_here * 16 + h * 4 + (other % 2) * 2 + k)

    loads = [
        pltpu.make_async_copy(src, dst, load.at[i])
        for i, (src, dst) in enumerate((
            (rf_hbm, rf_ref), (x_hbm, x_ref), (rb_hbm, rb_ref), (gb_hbm, gb_ref),
            (s_hbm, s_ref), (g_hbm, g_ref), (gf_hbm, gf_ref),
            (gw_ref.at[0, 0], w.at[0, k]), (uw_ref.at[0, 0], w.at[1, k]),
            (dw_ref.at[0, 0], w.at[2, k]),
        ))
    ]
    for copy in loads:
        copy.start()

    partner = (section, expert + 1 - 2 * k)

    barrier = pltpu.get_barrier_semaphore()
    def greet(d, carry):
        pl.semaphore_signal(
            barrier, inc=1, device_id=device((me + d) % group), device_id_type=MESH
        )
        return carry

    lax.fori_loop(1, group, greet, 0)

    def scatter(src, dst, ssem, rsem):
        def body(d, carry):
            n = (me + d) % group
            spot = n % half
            pltpu.make_async_remote_copy(
                src_ref=src(n, spot // 8, 2 * (n // half) + spot % 2),
                dst_ref=dst, send_sem=ssem.at[n], recv_sem=rsem.at[me],
                device_id=device(n), device_id_type=MESH,
            ).start()
            return carry

        lax.fori_loop(1, group, body, 0)

    def gathered(src, dst, ssem, rsem):
        def body(d, carry):
            n = (me + d) % group
            pltpu.make_async_remote_copy(
                src_ref=src, dst_ref=dst(n), send_sem=ssem.at[n], recv_sem=rsem.at[n],
                device_id=device(n), device_id_type=MESH,
            ).wait_recv()
            return carry

        lax.fori_loop(1, group, body, 0)

    def drained(src, dst, ssem, rsem):
        def body(d, carry):
            n = (me + d) % group
            pltpu.make_async_remote_copy(
                src_ref=src, dst_ref=dst, send_sem=ssem.at[n], recv_sem=rsem.at[n],
                device_id=device(n), device_id_type=MESH,
            ).wait_send()
            return carry

        lax.fori_loop(1, group, body, 0)

    def quad_copy(src, dst, ssem, rsem, d):
        return pltpu.make_async_remote_copy(
            src_ref=src, dst_ref=dst, send_sem=ssem.at[d], recv_sem=rsem.at[d],
            device_id=quad_device((q + d) % 4), device_id_type=MESH,
        )

    loads[0].wait()
    picks_f = [chosen_of(rf_ref[...], e, CAP).astype(BF16) for e in range(flight)]
    loads[1].wait()
    for e in range(flight):
        pick = picks_f[e]
        for part in range(4):
            cols = slice(part * chunk, (part + 1) * chunk)
            send_f[e, part] = jnp.dot(pick, x_ref[:, cols], preferred_element_type=F32).astype(BF16)

    weight_copies = [
        pltpu.make_async_remote_copy(
            src_ref=ref.at[0, 0], dst_ref=w.at[i, k], send_sem=w_s.at[i], recv_sem=w_r.at[i],
            device_id=partner, device_id_type=MESH,
        )
        for i, ref in enumerate((gw_ref, uw_ref, dw_ref))
    ]

    @pl.when(k == 0)
    def _():
        pl.semaphore_wait(barrier, group - 1)
        pl.semaphore_signal(barrier, inc=1, device_id=partner, device_id_type=MESH)

    @pl.when(k == 1)
    def _():
        pl.semaphore_wait(barrier, group)
        pl.semaphore_signal(barrier, inc=1, device_id=partner, device_id_type=MESH)
        for copy in weight_copies:
            copy.start()

    scatter(lambda n, e, part: send_f.at[e, part], in_f.at[me], inf_s, inf_r)

    for copy in loads[2:6]:
        copy.wait()
    for e in range(flight):
        pick_f32 = chosen_of(rb_ref[...], e, CAP)
        pick = pick_f32.astype(BF16)
        weight = gate_of(rb_ref[...], gb_ref[...], e)
        gate = jnp.sum(pick_f32 * weight, axis=1, keepdims=True)
        for part in range(4):
            cols = slice(part * chunk, (part + 1) * chunk)
            send_b[e, part, 0] = jnp.dot(pick, s_ref[:, cols], preferred_element_type=F32).astype(BF16)
            picked = jnp.dot(pick, g_ref[:, cols], preferred_element_type=F32)
            send_b[e, part, 1] = (picked * gate).astype(BF16)
    scatter(lambda n, e, part: send_b.at[e, part], in_b.at[me], inb_s, inb_r)

    @pl.when(k == 0)
    def _():
        pl.semaphore_wait(barrier, 1)
        for copy in weight_copies:
            copy.start()

    in_f[me] = send_f[e_here, q]
    in_b[me] = send_b[e_here, q]
    for copy in loads[6:]:
        copy.wait()
    for copy in weight_copies:
        copy.wait_recv()

    def matrix(i):
        return w[i].reshape(chunk, HID)

    def flat(block):
        return block.astype(F32).reshape(group * CAP, chunk).astype(BF16)

    def reduce_part(p32, ps, pr, ssem, rsem):
        copies = [quad_copy(ps.at[(q + d) % 4], pr.at[d], ssem, rsem, d) for d in range(1, 4)]
        for copy in copies:
            copy.start()
        total = p32[q]
        for d in range(1, 4):
            copies[d - 1].wait_recv()
            total = total + pr[d].astype(F32)
        return total, copies

    def share(h_ref, value, ssem, rsem):
        h_ref[q] = value
        copies = [quad_copy(h_ref.at[q], h_ref.at[q], ssem, rsem, d) for d in range(1, 4)]
        for copy in copies:
            copy.start()
        for d in range(1, 4):
            quad_copy(h_ref.at[q], h_ref.at[(q - d + 4) % 4], ssem, rsem, d).wait_recv()
        return copies

    gathered(send_f.at[0, 0], lambda n: in_f.at[n], inf_s, inf_r)
    block = flat(in_f[...])
    for i in range(2):
        part = jnp.dot(block, matrix(i), preferred_element_type=F32).reshape(4, rows, HID)
        p32_f[:, :, i * HID:(i + 1) * HID] = part
        ps_f[:, :, i * HID:(i + 1) * HID] = part.astype(BF16)
    total, sent_pf = reduce_part(p32_f, ps_f, pr_f, pf_s, pf_r)
    a, b = total[:, :HID], total[:, HID:]
    sent_hf = share(h_f, (a * jax.nn.sigmoid(a) * b).astype(BF16), hf_s, hf_r)
    hidden = h_f[...].reshape(group * CAP, HID)
    o_f[...] = (
        lax.dot_general(hidden, matrix(2), NT, preferred_element_type=F32)
        .reshape(group, CAP, chunk).astype(BF16)
    )
    scatter(lambda n, e, part: o_f.at[n], r_f.at[c, e_here, h, x], of_s, of_r)
    r_f[c, e_here, h, x] = o_f[me]

    gathered(send_b.at[0, 0], lambda n: in_b.at[n], inb_s, inb_r)
    block = flat(in_b[:, 0])
    for i in range(3):
        if i == 2:
            block = flat(in_b[:, 1])
        part = jnp.dot(block, matrix(i), preferred_element_type=F32).reshape(4, rows, HID)
        p32_b[:, :, i * HID:(i + 1) * HID] = part
        ps_b[:, :, i * HID:(i + 1) * HID] = part.astype(BF16)
    total, sent_pb = reduce_part(p32_b, ps_b, pr_b, pb_s, pb_r)
    a, b, d_hidden = total[:, :HID], total[:, HID:2 * HID], total[:, 2 * HID:]
    sigma = jax.nn.sigmoid(a)
    d_gate = (d_hidden * b * (sigma * (1.0 + a * (1.0 - sigma)))).astype(BF16)
    d_up = (d_hidden * (a * sigma)).astype(BF16)
    sent_hb = share(h_b, jnp.concatenate([d_gate, d_up], axis=1), hb_s, hb_r)
    both = h_b[...].reshape(group * CAP, 2 * HID)
    back = lax.dot_general(both[:, :HID], matrix(0), NT, preferred_element_type=F32)
    back = back + lax.dot_general(both[:, HID:], matrix(1), NT, preferred_element_type=F32)
    o_b[...] = back.reshape(group, CAP, chunk).astype(BF16)
    scatter(lambda n, e, part: o_b.at[n], r_b.at[c, e_here, h, x], ob_s, ob_r)
    r_b[c, e_here, h, x] = o_b[me]

    def combine(routes, gates, base, returned, out, out_hbm, weighted):
        picks = []
        stores = []
        for e in range(flight):
            tokens = routes.shape[1]
            chosen = chosen_of(routes[...], e, SLICES * CAP).astype(BF16)
            chosen = lax.dot_general(eye(tokens, BF16), chosen, NT, preferred_element_type=F32)
            gate = None
            if weighted:
                gate = lax.dot_general(
                    eye(tokens, F32), jnp.broadcast_to(gate_of(routes[...], gates[...], e), (CAP, tokens)),
                    NT, precision=lax.Precision.HIGHEST, preferred_element_type=F32,
                )[:, :1]
            picks.append((chosen.astype(BF16), gate))
        for part in range(4):
            cols = slice(part * chunk, (part + 1) * chunk)
            total = base[:, cols].astype(F32)
            for e in range(flight):
                chosen, weight = picks[e]
                piece = returned[part // 2, e, :, part % 2].astype(F32)
                piece = piece.reshape(SLICES * CAP, chunk).astype(BF16)
                term = jnp.dot(chosen, piece, preferred_element_type=F32)
                total = total + (term * weight if weighted else term)
            out[:, cols] = total.astype(BF16)
            stores.append(pltpu.make_async_copy(
                out.at[:, cols], out_hbm.at[:, cols], store.at[0 if weighted else 1, part]
            ))
            stores[-1].start()
        return stores

    def slot_of(buffer):
        return lambda n: buffer.at[n // half, n % half // 8, n % half // 2 % 4, n % 2]

    gathered(o_f.at[0], slot_of(r_f), of_s, of_r)
    stores = combine(rf_ref, gf_ref, x_ref, r_f, of_ref, of_hbm, True)
    gathered(o_b.at[0], slot_of(r_b), ob_s, ob_r)
    stores += combine(rb_ref, gb_ref, g_ref, r_b, ob_ref, ob_hbm, False)

    drained(send_f.at[0, 0], in_f.at[0], inf_s, inf_r)
    drained(send_b.at[0, 0], in_b.at[0], inb_s, inb_r)
    drained(o_f.at[0], r_f.at[0, 0, 0, 0], of_s, of_r)
    drained(o_b.at[0], r_b.at[0, 0, 0, 0], ob_s, ob_r)
    for copy in weight_copies + sent_pf + sent_hf + sent_pb + sent_hb:
        copy.wait_send()
    for copy in stores:
        copy.wait()


def solution(mesh):
    n_expert, n_section = mesh.shape["expert"], mesh.shape["section"]
    flight, group = n_expert // 16, n_expert
    tokens_spec = P(("section", "expert"), None)
    weight_spec = P("section", "expert", None, None)

    def per_device(*args):
        x = args[0]
        args = args[:3] + tuple(a.T for a in args[3:7]) + args[7:]
        chunk = x.shape[1] // 4
        rows = group // 4 * CAP
        hbm = pl.BlockSpec(memory_space=pltpu.HBM)
        dma = pltpu.SemaphoreType.DMA
        scratch = [
            pltpu.VMEM(x.shape, BF16), pltpu.VMEM(x.shape, BF16), pltpu.VMEM(x.shape, BF16),
            *[pltpu.VMEM(a.shape, a.dtype) for a in args[3:7]],
            dma((10,)),
            pltpu.VMEM(x.shape, BF16), pltpu.VMEM(x.shape, BF16), dma((2, 4)),
            pltpu.VMEM((flight, 4, CAP, chunk), BF16),
            pltpu.VMEM((flight, 4, 2, CAP, chunk), BF16),
            pltpu.VMEM((group, CAP, chunk), BF16),
            pltpu.VMEM((group, 2, CAP, chunk), BF16),
            pltpu.VMEM((3, 2, chunk // 2, HID), BF16),
            pltpu.VMEM((4, rows, 2 * HID), F32),
            pltpu.VMEM((4, rows, 3 * HID), F32),
            pltpu.VMEM((4, rows, 2 * HID), BF16),
            pltpu.VMEM((4, rows, 3 * HID), BF16),
            pltpu.VMEM((4, rows, 2 * HID), BF16),
            pltpu.VMEM((4, rows, 3 * HID), BF16),
            pltpu.VMEM((4, rows, HID), BF16),
            pltpu.VMEM((4, rows, 2 * HID), BF16),
            pltpu.VMEM((group, CAP, chunk), BF16),
            pltpu.VMEM((group, CAP, chunk), BF16),
            pltpu.VMEM((2, flight, SLICES, 2, CAP, chunk), BF16),
            pltpu.VMEM((2, flight, SLICES, 2, CAP, chunk), BF16),
            dma((3,)), dma((3,)),
            dma((group,)), dma((group,)), dma((group,)), dma((group,)),
            dma((4,)), dma((4,)), dma((4,)), dma((4,)),
            dma((4,)), dma((4,)), dma((4,)), dma((4,)),
            dma((group,)), dma((group,)), dma((group,)), dma((group,)),
        ]
        out = jax.ShapeDtypeStruct(x.shape, BF16)
        forward, gradient = pl.pallas_call(
            functools.partial(kernel, n_expert, chunk),
            out_shape=(out, out),
            in_specs=[hbm] * 10,
            out_specs=(hbm, hbm),
            scratch_shapes=scratch,
            compiler_params=pltpu.CompilerParams(
                collective_id=0, has_side_effects=True, vmem_limit_bytes=58 * 1024 * 1024
            ),
        )(*args)
        if n_section > 2:
            onward = [(i, (i + 2) % n_section) for i in range(n_section)]
            back = [(i, (i - 2) % n_section) for i in range(n_section)]
            forward = lax.ppermute(forward, "section", onward)
            gradient = lax.ppermute(gradient, "section", back)
        return forward, gradient

    return jax.shard_map(
        per_device,
        mesh=mesh,
        in_specs=(tokens_spec,) * 7 + (weight_spec,) * 3,
        out_specs=(tokens_spec, tokens_spec),
        check_vma=False,
    )
```

```python
import functools

import jax
import jax.numpy as jnp
from jax import lax
from jax.experimental import pallas as pl
from jax.experimental.pallas import tpu as pltpu
from jax.sharding import PartitionSpec as P

CAP = 8
SLICES = 4
HID = 256
MESH = pl.DeviceIdType.MESH
F32 = jnp.float32
BF16 = jnp.bfloat16
NT = (((1,), (1,)), ((), ()))


def eye(size, dtype):
    rows = lax.broadcasted_iota(jnp.int32, (size, size), 0)
    cols = lax.broadcasted_iota(jnp.int32, (size, size), 1)
    return (rows == cols).astype(F32).astype(dtype)


def chosen_of(routes, e, height):
    tokens = routes.shape[1]
    member = jnp.max((routes == e).astype(F32), axis=0, keepdims=True)
    tri = (
        lax.broadcasted_iota(jnp.int32, (tokens, tokens), 0)
        >= lax.broadcasted_iota(jnp.int32, (tokens, tokens), 1)
    ).astype(F32).astype(BF16)
    wide = jnp.broadcast_to(member, (height, tokens))
    position = lax.dot_general(wide.astype(BF16), tri, NT, preferred_element_type=F32) - 1.0
    slot = (lax.broadcasted_iota(jnp.int32, (height, tokens), 0) % CAP).astype(F32)
    return jnp.where((position == slot) & (wide > 0), 1.0, 0.0)


def gate_of(routes, gates, e):
    return jnp.sum(jnp.where(routes == e, gates, 0.0), axis=0, keepdims=True)


def kernel(
    n_expert, chunk,
    x_hbm, s_hbm, g_hbm, rf_hbm, gf_hbm, rb_hbm, gb_hbm, gw_ref, uw_ref, dw_ref,
    of_hbm, ob_hbm,
    x_ref, s_ref, g_ref, rf_ref, gf_ref, rb_ref, gb_ref, load, of_ref, ob_ref, store,
    send_f, send_b, in_f, in_b, w, p32_f, p32_b, ps_f, ps_b, pr_f, pr_b, h_f, h_b,
    o_f, o_b, r_f, r_b,
    w_s, w_r, inf_s, inf_r, inb_s, inb_r, pf_s, pf_r, pb_s, pb_r, hf_s, hf_r, hb_s, hb_r,
    of_s, of_r, ob_s, ob_r,
):
    flight = n_expert // 16
    group = n_expert
    half = group // 2
    rows = group // 4 * CAP
    section, expert = lax.axis_index("section"), lax.axis_index("expert")
    layer, c, k = section // 2, section % 2, expert % 2
    place = expert // 2
    me = c * half + place
    x = place % 2
    h = place // 2 % 4
    e_here = place // 8
    q = 2 * c + x

    def device(n):
        return (layer * 2 + n // half, (n % half) * 2 + k)

    def quad_device(other):
        return (layer * 2 + other // 2, e_here * 16 + h * 4 + (other % 2) * 2 + k)

    loads = [
        pltpu.make_async_copy(src, dst, load.at[i])
        for i, (src, dst) in enumerate((
            (rf_hbm, rf_ref), (x_hbm, x_ref), (rb_hbm, rb_ref), (gb_hbm, gb_ref),
            (s_hbm, s_ref), (g_hbm, g_ref), (gf_hbm, gf_ref),
            (gw_ref.at[0, 0], w.at[0, k]), (uw_ref.at[0, 0], w.at[1, k]),
            (dw_ref.at[0, 0], w.at[2, k]),
        ))
    ]
    for copy in loads:
        copy.start()

    partner = (section, expert + 1 - 2 * k)

    barrier = pltpu.get_barrier_semaphore()
    def greet(d, carry):
        pl.semaphore_signal(
            barrier, inc=1, device_id=device((me + d) % group), device_id_type=MESH
        )
        return carry

    lax.fori_loop(1, group, greet, 0)

    def scatter(src, dst, ssem, rsem):
        def body(d, carry):
            n = (me + d) % group
            spot = n % half
            pltpu.make_async_remote_copy(
                src_ref=src(n, spot // 8, 2 * (n // half) + spot % 2),
                dst_ref=dst, send_sem=ssem.at[n], recv_sem=rsem.at[me],
                device_id=device(n), device_id_type=MESH,
            ).start()
            return carry

        lax.fori_loop(1, group, body, 0)

    def gathered(src, dst, ssem, rsem):
        def body(d, carry):
            n = (me + d) % group
            pltpu.make_async_remote_copy(
                src_ref=src, dst_ref=dst(n), send_sem=ssem.at[n], recv_sem=rsem.at[n],
                device_id=device(n), device_id_type=MESH,
            ).wait_recv()
            return carry

        lax.fori_loop(1, group, body, 0)

    def drained(src, dst, ssem, rsem):
        def body(d, carry):
            n = (me + d) % group
            pltpu.make_async_remote_copy(
                src_ref=src, dst_ref=dst, send_sem=ssem.at[n], recv_sem=rsem.at[n],
                device_id=device(n), device_id_type=MESH,
            ).wait_send()
            return carry

        lax.fori_loop(1, group, body, 0)

    def quad_copy(src, dst, ssem, rsem, d):
        return pltpu.make_async_remote_copy(
            src_ref=src, dst_ref=dst, send_sem=ssem.at[d], recv_sem=rsem.at[d],
            device_id=quad_device((q + d) % 4), device_id_type=MESH,
        )

    loads[0].wait()
    picks_f = [chosen_of(rf_ref[...], e, CAP).astype(BF16) for e in range(flight)]
    loads[1].wait()
    for e in range(flight):
        pick = picks_f[e]
        for part in range(4):
            cols = slice(part * chunk, (part + 1) * chunk)
            send_f[e, part] = jnp.dot(pick, x_ref[:, cols], preferred_element_type=F32).astype(BF16)

    weight_copies = [
        pltpu.make_async_remote_copy(
            src_ref=ref.at[0, 0], dst_ref=w.at[i, k], send_sem=w_s.at[i], recv_sem=w_r.at[i],
            device_id=partner, device_id_type=MESH,
        )
        for i, ref in enumerate((gw_ref, uw_ref, dw_ref))
    ]

    @pl.when(k == 0)
    def _():
        pl.semaphore_wait(barrier, group - 1)
        pl.semaphore_signal(barrier, inc=1, device_id=partner, device_id_type=MESH)

    @pl.when(k == 1)
    def _():
        pl.semaphore_wait(barrier, group)
        pl.semaphore_signal(barrier, inc=1, device_id=partner, device_id_type=MESH)
        for copy in weight_copies:
            copy.start()

    scatter(lambda n, e, part: send_f.at[e, part], in_f.at[me], inf_s, inf_r)

    for copy in loads[2:6]:
        copy.wait()
    for e in range(flight):
        pick_f32 = chosen_of(rb_ref[...], e, CAP)
        pick = pick_f32.astype(BF16)
        weight = gate_of(rb_ref[...], gb_ref[...], e)
        gate = jnp.sum(pick_f32 * weight, axis=1, keepdims=True)
        for part in range(4):
            cols = slice(part * chunk, (part + 1) * chunk)
            send_b[e, part, 0] = jnp.dot(pick, s_ref[:, cols], preferred_element_type=F32).astype(BF16)
            picked = jnp.dot(pick, g_ref[:, cols], preferred_element_type=F32)
            send_b[e, part, 1] = (picked * gate).astype(BF16)
    scatter(lambda n, e, part: send_b.at[e, part], in_b.at[me], inb_s, inb_r)

    @pl.when(k == 0)
    def _():
        pl.semaphore_wait(barrier, 1)
        for copy in weight_copies:
            copy.start()

    in_f[me] = send_f[e_here, q]
    in_b[me] = send_b[e_here, q]
    for copy in loads[6:]:
        copy.wait()
    for copy in weight_copies:
        copy.wait_recv()

    def matrix(i):
        return w[i].reshape(chunk, HID)

    def flat(block):
        return block.astype(F32).reshape(group * CAP, chunk).astype(BF16)

    def reduce_part(p32, ps, pr, ssem, rsem):
        copies = [quad_copy(ps.at[(q + d) % 4], pr.at[d], ssem, rsem, d) for d in range(1, 4)]
        for copy in copies:
            copy.start()
        total = p32[q]
        for d in range(1, 4):
            copies[d - 1].wait_recv()
            total = total + pr[d].astype(F32)
        return total, copies

    def share(h_ref, value, ssem, rsem):
        h_ref[q] = value
        copies = [quad_copy(h_ref.at[q], h_ref.at[q], ssem, rsem, d) for d in range(1, 4)]
        for copy in copies:
            copy.start()
        for d in range(1, 4):
            quad_copy(h_ref.at[q], h_ref.at[(q - d + 4) % 4], ssem, rsem, d).wait_recv()
        return copies

    gathered(send_f.at[0, 0], lambda n: in_f.at[n], inf_s, inf_r)
    block = flat(in_f[...])
    for i in range(2):
        part = jnp.dot(block, matrix(i), preferred_element_type=F32).reshape(4, rows, HID)
        p32_f[:, :, i * HID:(i + 1) * HID] = part
        ps_f[:, :, i * HID:(i + 1) * HID] = part.astype(BF16)
    total, sent_pf = reduce_part(p32_f, ps_f, pr_f, pf_s, pf_r)
    a, b = total[:, :HID], total[:, HID:]
    sent_hf = share(h_f, (a * jax.nn.sigmoid(a) * b).astype(BF16), hf_s, hf_r)
    hidden = h_f[...].reshape(group * CAP, HID)
    o_f[...] = (
        lax.dot_general(hidden, matrix(2), NT, preferred_element_type=F32)
        .reshape(group, CAP, chunk).astype(BF16)
    )
    scatter(lambda n, e, part: o_f.at[n], r_f.at[c, e_here, h, x], of_s, of_r)
    r_f[c, e_here, h, x] = o_f[me]

    gathered(send_b.at[0, 0], lambda n: in_b.at[n], inb_s, inb_r)
    block = flat(in_b[:, 0])
    for i in range(3):
        if i == 2:
            block = flat(in_b[:, 1])
        part = jnp.dot(block, matrix(i), preferred_element_type=F32).reshape(4, rows, HID)
        p32_b[:, :, i * HID:(i + 1) * HID] = part
        ps_b[:, :, i * HID:(i + 1) * HID] = part.astype(BF16)
    total, sent_pb = reduce_part(p32_b, ps_b, pr_b, pb_s, pb_r)
    a, b, d_hidden = total[:, :HID], total[:, HID:2 * HID], total[:, 2 * HID:]
    sigma = jax.nn.sigmoid(a)
    d_gate = (d_hidden * b * (sigma * (1.0 + a * (1.0 - sigma)))).astype(BF16)
    d_up = (d_hidden * (a * sigma)).astype(BF16)
    sent_hb = share(h_b, jnp.concatenate([d_gate, d_up], axis=1), hb_s, hb_r)
    both = h_b[...].reshape(group * CAP, 2 * HID)
    back = lax.dot_general(both[:, :HID], matrix(0), NT, preferred_element_type=F32)
    back = back + lax.dot_general(both[:, HID:], matrix(1), NT, preferred_element_type=F32)
    o_b[...] = back.reshape(group, CAP, chunk).astype(BF16)
    scatter(lambda n, e, part: o_b.at[n], r_b.at[c, e_here, h, x], ob_s, ob_r)
    r_b[c, e_here, h, x] = o_b[me]

    def picks_of(routes, gates, weighted):
        picks = []
        for e in range(flight):
            tokens = routes.shape[1]
            chosen = chosen_of(routes[...], e, SLICES * CAP).astype(BF16)
            chosen = lax.dot_general(eye(tokens, BF16), chosen, NT, preferred_element_type=F32)
            gate = None
            if weighted:
                gate = lax.dot_general(
                    eye(tokens, F32), jnp.broadcast_to(gate_of(routes[...], gates[...], e), (CAP, tokens)),
                    NT, precision=lax.Precision.HIGHEST, preferred_element_type=F32,
                )[:, :1]
            picks.append((chosen.astype(BF16), gate))
        return picks

    def combine(picks, base, returned, out, out_hbm, weighted):
        stores = []
        for part in range(4):
            cols = slice(part * chunk, (part + 1) * chunk)
            total = base[:, cols].astype(F32)
            for e in range(flight):
                chosen, weight = picks[e]
                piece = returned[part // 2, e, :, part % 2].astype(F32)
                piece = piece.reshape(SLICES * CAP, chunk).astype(BF16)
                term = jnp.dot(chosen, piece, preferred_element_type=F32)
                total = total + (term * weight if weighted else term)
            out[:, cols] = total.astype(BF16)
            stores.append(pltpu.make_async_copy(
                out.at[:, cols], out_hbm.at[:, cols], store.at[0 if weighted else 1, part]
            ))
            stores[-1].start()
        return stores

    def slot_of(buffer):
        return lambda n: buffer.at[n // half, n % half // 8, n % half // 2 % 4, n % 2]

    picks_f = picks_of(rf_ref, gf_ref, True)
    picks_b = picks_of(rb_ref, gb_ref, False)
    gathered(o_f.at[0], slot_of(r_f), of_s, of_r)
    stores = combine(picks_f, x_ref, r_f, of_ref, of_hbm, True)
    drained(send_f.at[0, 0], in_f.at[0], inf_s, inf_r)
    drained(send_b.at[0, 0], in_b.at[0], inb_s, inb_r)
    drained(o_f.at[0], r_f.at[0, 0, 0, 0], of_s, of_r)
    for copy in weight_copies + sent_pf + sent_hf + sent_pb + sent_hb:
        copy.wait_send()
    gathered(o_b.at[0], slot_of(r_b), ob_s, ob_r)
    stores += combine(picks_b, g_ref, r_b, ob_ref, ob_hbm, False)
    drained(o_b.at[0], r_b.at[0, 0, 0, 0], ob_s, ob_r)
    for copy in stores:
        copy.wait()


def solution(mesh):
    n_expert, n_section = mesh.shape["expert"], mesh.shape["section"]
    flight, group = n_expert // 16, n_expert
    tokens_spec = P(("section", "expert"), None)
    weight_spec = P("section", "expert", None, None)

    def per_device(*args):
        x = args[0]
        args = args[:3] + tuple(a.T for a in args[3:7]) + args[7:]
        chunk = x.shape[1] // 4
        rows = group // 4 * CAP
        hbm = pl.BlockSpec(memory_space=pltpu.HBM)
        dma = pltpu.SemaphoreType.DMA
        scratch = [
            pltpu.VMEM(x.shape, BF16), pltpu.VMEM(x.shape, BF16), pltpu.VMEM(x.shape, BF16),
            *[pltpu.VMEM(a.shape, a.dtype) for a in args[3:7]],
            dma((10,)),
            pltpu.VMEM(x.shape, BF16), pltpu.VMEM(x.shape, BF16), dma((2, 4)),
            pltpu.VMEM((flight, 4, CAP, chunk), BF16),
            pltpu.VMEM((flight, 4, 2, CAP, chunk), BF16),
            pltpu.VMEM((group, CAP, chunk), BF16),
            pltpu.VMEM((group, 2, CAP, chunk), BF16),
            pltpu.VMEM((3, 2, chunk // 2, HID), BF16),
            pltpu.VMEM((4, rows, 2 * HID), F32),
            pltpu.VMEM((4, rows, 3 * HID), F32),
            pltpu.VMEM((4, rows, 2 * HID), BF16),
            pltpu.VMEM((4, rows, 3 * HID), BF16),
            pltpu.VMEM((4, rows, 2 * HID), BF16),
            pltpu.VMEM((4, rows, 3 * HID), BF16),
            pltpu.VMEM((4, rows, HID), BF16),
            pltpu.VMEM((4, rows, 2 * HID), BF16),
            pltpu.VMEM((group, CAP, chunk), BF16),
            pltpu.VMEM((group, CAP, chunk), BF16),
            pltpu.VMEM((2, flight, SLICES, 2, CAP, chunk), BF16),
            pltpu.VMEM((2, flight, SLICES, 2, CAP, chunk), BF16),
            dma((3,)), dma((3,)),
            dma((group,)), dma((group,)), dma((group,)), dma((group,)),
            dma((4,)), dma((4,)), dma((4,)), dma((4,)),
            dma((4,)), dma((4,)), dma((4,)), dma((4,)),
            dma((group,)), dma((group,)), dma((group,)), dma((group,)),
        ]
        out = jax.ShapeDtypeStruct(x.shape, BF16)
        forward, gradient = pl.pallas_call(
            functools.partial(kernel, n_expert, chunk),
            out_shape=(out, out),
            in_specs=[hbm] * 10,
            out_specs=(hbm, hbm),
            scratch_shapes=scratch,
            compiler_params=pltpu.CompilerParams(
                collective_id=0, has_side_effects=True, vmem_limit_bytes=58 * 1024 * 1024
            ),
        )(*args)
        if n_section > 2:
            onward = [(i, (i + 2) % n_section) for i in range(n_section)]
            back = [(i, (i - 2) % n_section) for i in range(n_section)]
            forward = lax.ppermute(forward, "section", onward)
            gradient = lax.ppermute(gradient, "section", back)
        return forward, gradient

    return jax.shard_map(
        per_device,
        mesh=mesh,
        in_specs=(tokens_spec,) * 7 + (weight_spec,) * 3,
        out_specs=(tokens_spec, tokens_spec),
        check_vma=False,
    )
```
